32 devices in a mesh: section: 4 (over y, x), fork: 8 (over z, core).
Axes of the slice: x: 2, y: 2, z: 4, core: 2. Of those that a mesh axis runs over, the one named last changes fastest.
Arguments:
- arriving: bfloat16 [4, 8, 128, 4096], P('section', 'fork'), may hold values from -6 to 6
- saved_input: bfloat16 [4, 8, 128, 4096], P('section', 'fork'), may hold values from -6 to 6
- returning: bfloat16 [4, 8, 128, 4096], P('section', 'fork'), may hold values from -6 to 6
- prompt_cache: bfloat16 [4, 2, 512, 512], P('section', None, 'fork'), may hold values from -20 to 20
- fresh_cache: bfloat16 [4, 8, 2, 128, 512], P('section', 'fork'), may hold values from -6 to 6
- back_cache: bfloat16 [4, 8, 2, 128, 512], P('section', 'fork'), may hold values from -6 to 6
- query_gain: float32 [4, 4096], P('section'), may hold values from 0.25 to 1.75
- block_tables: int32 [8, 16], P('fork'), may hold values from 0 to 31, as said below
- fresh_lengths: int32 [8], P('fork'), may hold values from 32 to 128
- back_lengths: int32 [8], P('fork'), may hold values from 32 to 128
Outputs:
- section_output: bfloat16 [4, 8, 128, 4096], P('section', 'fork')
- input_grad: bfloat16 [4, 8, 128, 4096], P('section', 'fork')
- prompt_grad: float32 [4, 2, 512, 512], P('section', None, 'fork')
- completion_grad: float32 [4, 8, 2, 128, 512], P('section', 'fork')
- gain_grad: float32 [4, 4096], P('section')
The draws below stay inside these ranges and needn't reach their ends.
Inputs may be any that keep to these rules, and one draw needn't show every extreme that they name: `block_tables`: completions 0 to 3 read one prompt and the others a second one: each row lists that prompt's 16 pool blocks in order, the same row for all completions of a prompt; the two prompts' blocks are distinct and together fill the pool.
All inputs are finite; a program needn't handle non-finite values.
Results may differ from the reference program's by a relative error of at most 0.0023.
The reference program's roundings to bfloat16 on the way count: a program that leaves them out, or rounds other values in their place, can miss the bound.
Values may be sent and summed in bfloat16 or wider, within the bound.
A program may use at most 128 MiB of HBM per device.

```python
import jax
import jax.numpy as jnp
from jax import lax

KV = 4
HD = 128
BLOCK = 16
COMP = 128
W = 4096
SECTIONS = 4
FORKS = 8
POOL = 32
NB = 16


def activation_draw(key, salt):
    shape = (SECTIONS, FORKS, COMP, W)
    base = jax.random.normal(jax.random.fold_in(key, salt), shape, jnp.float32)
    return jnp.clip(base, -6.0, 6.0)


def draw_arriving(key, part):
    return activation_draw(key, 101).astype(jnp.bfloat16)


def draw_saved_input(key, part):
    return activation_draw(key, 202).astype(jnp.bfloat16)


def draw_prompt_cache(key, part):
    shape = (SECTIONS, 2, POOL * BLOCK, KV * HD)
    base = jax.random.normal(jax.random.fold_in(key, 303), shape, jnp.float32)
    return jnp.clip(base, -6.0, 6.0).astype(jnp.bfloat16)


def draw_block_tables(key, part):
    shuffled = jax.random.permutation(jax.random.fold_in(key, 17), POOL)
    completion = jnp.arange(FORKS, dtype=jnp.int32)
    prompt_index = completion // (FORKS // 2)
    places = prompt_index[:, None] * NB + jnp.arange(NB, dtype=jnp.int32)[None, :]
    return shuffled[places].astype(jnp.int32)


def set_ends(entries, stream_key, low, top_value):
    longest = entries.shape.index(max(entries.shape))
    spots = []
    for shift in (0, 1):
        where = [jax.random.randint(jax.random.fold_in(stream_key, axis), (), 0, length) for axis, length in enumerate(entries.shape)]
        where[longest] = (where[longest] + shift) % entries.shape[longest]
        spots.append(tuple(where))
    return entries.at[spots[0]].set(low).at[spots[1]].set(top_value)


def steps_of(stream_key, dims, cuts, low, largest):
    def one(axis_at, parts):
        heights = jax.random.uniform(jax.random.fold_in(jax.random.fold_in(stream_key, 6), axis_at), (parts,), jnp.float32, low / len(cuts), largest / len(cuts))
        return jnp.repeat(jnp.exp(heights), dims[axis_at] // parts).reshape((-1,) + (1,) * (len(dims) - axis_at - 1))

    level = one(*cuts[0])
    for cut in cuts[1:]:
        level = level * one(*cut)
    return level


def bell_draw(own_key, extent, spread, reach, split=(), kind=jnp.bfloat16):
    entries = spread * jax.random.normal(own_key, extent, jnp.float32)
    if split:
        entries = entries * steps_of(own_key, extent, split, -0.22, 0.18)
    return jnp.clip(entries, -reach, reach).astype(kind)


def setup_inputs(seed: int = 0) -> dict:
    splits = jax.random.split(jax.random.key(seed), 11)
    return {
        "arriving": draw_arriving(jax.random.fold_in(splits[10], 71), 0),
        "saved_input": draw_saved_input(jax.random.fold_in(splits[10], 71), 0),
        "returning": bell_draw(splits[2], (SECTIONS, FORKS, COMP, W), 1.0, 6.0, ((0, 4), (1, 8))),
        "prompt_cache": draw_prompt_cache(jax.random.fold_in(splits[10], 71), 0),
        "fresh_cache": bell_draw(splits[4], (SECTIONS, FORKS, 2, COMP, KV * HD), 1.0, 6.0, ((0, 4), (1, 8))),
        "back_cache": bell_draw(splits[5], (SECTIONS, FORKS, 2, COMP, KV * HD), 1.0, 6.0, ((0, 4), (1, 8))),
        "query_gain": jnp.clip(1.0 + 0.15 * jax.random.normal(splits[6], (SECTIONS, W), jnp.float32), 0.25, 1.75),
        "block_tables": draw_block_tables(jax.random.fold_in(splits[10], 71), 0),
        "fresh_lengths": set_ends(jax.random.randint(splits[8], (FORKS,), COMP // 4, COMP + 1), jax.random.fold_in(splits[8], 1), COMP // 4, COMP).astype(jnp.int32),
        "back_lengths": set_ends(jax.random.randint(splits[9], (FORKS,), COMP // 4, COMP + 1), jax.random.fold_in(splits[9], 1), COMP // 4, COMP).astype(jnp.int32),
    }


epsilon = 1e-06
masked_score = -1e+30

def normed(x_rows, gain_row):
    floated = x_rows.astype(jnp.float32)
    inverse = lax.rsqrt(lax.optimization_barrier(jnp.mean(floated * floated, axis=-1, keepdims=True)) + epsilon)
    queries = lax.optimization_barrier((floated * inverse * gain_row).astype(jnp.bfloat16))
    return (queries, floated, inverse)

def visible_keys(row_count, prompt_count, length):
    places = jnp.arange(row_count, dtype=jnp.int32)
    recent = (places[None, :] <= places[:, None]) & (places[None, :] < length)
    return jnp.concatenate([jnp.ones((row_count, prompt_count), dtype=bool), recent], axis=1)

def by_group(array):
    return array.reshape(array.shape[0], KV, -1).transpose(1, 0, 2)

def softmax_rows(q_group, k_group, key_mask):
    row_count = q_group.shape[0]
    head_rows = q_group.reshape(row_count, -1, HD).astype(jnp.float32)
    scores = jnp.einsum('ihd,td->hit', head_rows, k_group.astype(jnp.float32)) * HD ** (-0.5)
    scores = jnp.where(key_mask[None], scores, masked_score)
    shifted = jnp.exp(scores - lax.optimization_barrier(jnp.max(scores, axis=-1, keepdims=True)))
    return (shifted / lax.optimization_barrier(jnp.sum(shifted, axis=-1, keepdims=True)), head_rows)

def forward_layer(x_rows, gain_row, prompt_keys, prompt_values, own_cache, length):
    queries, floated, inverse = normed(x_rows, gain_row)
    row_count = x_rows.shape[0]
    all_keys = jnp.concatenate([prompt_keys, own_cache[0]], axis=0)
    all_values = jnp.concatenate([prompt_values, own_cache[1]], axis=0)
    key_mask = visible_keys(row_count, prompt_keys.shape[0], length)

    def per_group(pieces):
        q_group, k_group, v_group = pieces
        chances, head_rows = softmax_rows(q_group, k_group, key_mask)
        rounded = lax.optimization_barrier(chances.astype(jnp.bfloat16)).astype(jnp.float32)
        return jnp.einsum('hit,td->ihd', rounded, v_group.astype(jnp.float32)).reshape(row_count, -1)
    results = lax.map(per_group, (by_group(queries), by_group(all_keys), by_group(all_values)))
    attended = results.transpose(1, 0, 2).reshape(row_count, -1)
    valid_rows = (jnp.arange(row_count, dtype=jnp.int32) < length).astype(jnp.float32)[:, None]
    return (floated + valid_rows * attended).astype(jnp.bfloat16)

def backward_layer(x_rows, gain_row, prompt_keys, prompt_values, own_cache, length, cotangent):
    queries, floated, inverse = normed(x_rows, gain_row)
    row_count = x_rows.shape[0]
    prompt_count = prompt_keys.shape[0]
    all_keys = jnp.concatenate([prompt_keys, own_cache[0]], axis=0)
    all_values = jnp.concatenate([prompt_values, own_cache[1]], axis=0)
    key_mask = visible_keys(row_count, prompt_count, length)
    valid_rows = (jnp.arange(row_count, dtype=jnp.int32) < length).astype(jnp.float32)[:, None]
    grad_float = cotangent.astype(jnp.float32)
    out_grad = lax.optimization_barrier((valid_rows * grad_float).astype(jnp.bfloat16))

    def per_group(pieces):
        q_group, k_group, v_group, d_group = pieces
        chances, head_rows = softmax_rows(q_group, k_group, key_mask)
        rounded = lax.optimization_barrier(chances.astype(jnp.bfloat16)).astype(jnp.float32)
        d_out = d_group.reshape(row_count, -1, HD).astype(jnp.float32)
        d_value = jnp.einsum('hit,ihd->td', rounded, d_out)
        d_weight = jnp.einsum('ihd,td->hit', d_out, v_group.astype(jnp.float32))
        row_delta = lax.optimization_barrier(jnp.sum(chances * d_weight, axis=-1, keepdims=True))
        d_score = (chances * (d_weight - row_delta) * HD ** (-0.5)).astype(jnp.bfloat16)
        d_score = lax.optimization_barrier(d_score).astype(jnp.float32)
        d_query = jnp.einsum('hit,td->ihd', d_score, k_group.astype(jnp.float32)).reshape(row_count, -1)
        d_key = jnp.einsum('hit,ihd->td', d_score, head_rows)
        return (d_query, d_key, d_value)
    d_query, d_key, d_value = lax.map(per_group, (by_group(queries), by_group(all_keys), by_group(all_values), by_group(out_grad)))
    d_query = d_query.transpose(1, 0, 2).reshape(row_count, -1)
    d_key = d_key.transpose(1, 0, 2).reshape(all_keys.shape[0], -1)
    d_value = d_value.transpose(1, 0, 2).reshape(all_keys.shape[0], -1)
    d_normed = d_query * gain_row
    d_input = inverse * d_normed - floated * inverse ** 3 * lax.optimization_barrier(jnp.mean(d_normed * floated, axis=-1, keepdims=True))
    gain_part = lax.optimization_barrier(jnp.sum(d_query * floated * inverse, axis=0))
    own_grad = jnp.stack([d_key[prompt_count:], d_value[prompt_count:]])
    shared_grad = jnp.stack([d_key[:prompt_count], d_value[:prompt_count]])
    return ((grad_float + d_input).astype(jnp.bfloat16), own_grad, shared_grad, gain_part)

def reference(arriving, saved_input, returning, prompt_cache, fresh_cache, back_cache, query_gain, block_tables, fresh_lengths, back_lengths):
    entering = jnp.roll(arriving, 1, axis=0)
    leaving = jnp.roll(returning, -1, axis=0)

    def section_step(unused, inputs):
        fresh_x, back_x, cotangents, block_pool, fresh_kv, back_kv, gain_row = inputs
        blocks = block_pool.reshape(2, -1, BLOCK, block_pool.shape[-1])

        def fork_step(running, member):
            pool_total, gain_total = running
            x_fresh, x_back, cot_rows, kv_fresh, kv_back, block_table, length_fresh, length_back = member
            picked = jnp.take(blocks, block_table, axis=1).reshape(2, -1, block_pool.shape[-1])
            out_fresh = forward_layer(x_fresh, gain_row, picked[0], picked[1], kv_fresh, length_fresh)
            out_back, own_grad, shared_grad, gain_part = backward_layer(x_back, gain_row, picked[0], picked[1], kv_back, length_back, cot_rows)
            pool_total = pool_total.at[:, block_table].add(shared_grad.reshape(2, block_table.shape[0], BLOCK, -1))
            return ((pool_total, gain_total + gain_part), (out_fresh, out_back, own_grad))
        start_state = (jnp.zeros(blocks.shape, jnp.float32), jnp.zeros(gain_row.shape, jnp.float32))
        (pool_total, gain_total), (out_fresh, out_back, own_grad) = lax.scan(fork_step, start_state, (fresh_x, back_x, cotangents, fresh_kv, back_kv, block_tables, fresh_lengths, back_lengths))
        return (unused, (out_fresh, out_back, pool_total.reshape(block_pool.shape), own_grad, gain_total))
    unused, results = lax.scan(section_step, jnp.zeros((), jnp.float32), (entering, saved_input, leaving, prompt_cache, fresh_cache, back_cache, query_gain))
    section_output, input_grad, prompt_grad, completion_grad, gain_grad = results
    return (section_output, input_grad, prompt_grad, completion_grad, gain_grad)
```

```python
import math

import jax
import jax.numpy as jnp
from jax import lax
from jax.experimental import pallas as pl
from jax.experimental.pallas import tpu as pltpu
from jax.sharding import PartitionSpec as P

KV = 4
HD = 128
BLOCK = 16


epsilon = 1e-06
masked_score = -1e30
scale = HD ** (-0.5)
exp_scale = scale * math.log2(math.e)
vmem_limit = 48 * 1024 * 1024


def shifted_2(value, axis, steps):
    count = lax.axis_size(axis)
    pairs = [(source, (source + steps) % count) for source in range(count)]
    return lax.ppermute(value, axis, pairs)


def gather_rows(table, pool, own, held, which):
    prompt_count = table.shape[0] * BLOCK

    @pl.loop(0, table.shape[0])
    def _(j):
        source = pl.multiple_of(table[j] * BLOCK, BLOCK)
        target = pl.multiple_of(j * BLOCK, BLOCK)
        held[pl.ds(target, BLOCK), :] = pool[which, pl.ds(source, BLOCK), :]

    held[prompt_count:, :] = own[which]


def norm_rows(x, gain, queries, inverses):
    rows = BLOCK

    @pl.loop(0, x.shape[0] // rows)
    def _(i):
        place = pl.ds(pl.multiple_of(i * rows, rows), rows)
        floated = x[place, :].astype(jnp.float32)
        inverse = lax.rsqrt(jnp.mean(floated * floated, axis=-1, keepdims=True) + epsilon)
        queries[place, :] = (floated * inverse * gain[...]).astype(jnp.bfloat16)
        if inverses is not None:
            inverses[place, :] = jnp.broadcast_to(inverse, (rows, HD))


def dot(a, b, left, right):
    return lax.dot_general(a, b, (((left,), (right,)), ((), ())), preferred_element_type=jnp.float32)


def key_mask(rows, length):
    key = lax.broadcasted_iota(jnp.int32, (rows, rows), 0)
    row = lax.broadcasted_iota(jnp.int32, (rows, rows), 1)
    return (key <= row) & (key < length)


def chances_of(q_head, keys, mask):
    rows = mask.shape[0]
    scores = dot(keys, q_head, 1, 1)
    prompt = scores[:-rows]
    recent = jnp.where(mask, scores[-rows:], masked_score)
    top = jnp.maximum(jnp.max(prompt, axis=0, keepdims=True), jnp.max(recent, axis=0, keepdims=True))
    prompt = jnp.exp2((prompt - top) * exp_scale)
    recent = jnp.exp2((recent - top) * exp_scale)
    total = jnp.sum(prompt, axis=0, keepdims=True) + jnp.sum(recent, axis=0, keepdims=True)
    return jnp.concatenate([prompt, recent], axis=0) * (1.0 / total)


def forward_kernel(table, length, x, gain, pool, own, out, queries, keys, values):
    rows, width = x.shape
    group = width // KV
    gather_rows(table, pool, own, keys, 0)
    gather_rows(table, pool, own, values, 1)
    norm_rows(x, gain, queries, None)
    mask = key_mask(rows, length[0])
    valid = (lax.broadcasted_iota(jnp.int32, (rows, HD), 0) < length[0]).astype(jnp.float32)

    @pl.loop(0, KV)
    def _(g):
        columns = pl.ds(pl.multiple_of(g * HD, HD), HD)
        k_group = keys[:, columns]
        v_group = values[:, columns]
        for h in range(group // HD):
            place = pl.ds(pl.multiple_of(g * group + h * HD, HD), HD)
            chances = chances_of(queries[:, place], k_group, mask)
            attended = dot(v_group, chances.astype(jnp.bfloat16), 0, 0).T
            out[:, place] = (x[:, place].astype(jnp.float32) + valid * attended).astype(out.dtype)


def backward_kernel(
    table, length, x, gain, pool, own, cotangent,
    input_grad, pool_grad, own_grad, gain_grad,
    queries, inverses, keys, values, outs, weights, d_scores, d_queries, d_key, d_value,
):
    rows, width = x.shape
    group = width // KV
    prompt_count = table.shape[0] * BLOCK
    pool_grad[...] = jnp.zeros_like(pool_grad)
    gather_rows(table, pool, own, keys, 0)
    gather_rows(table, pool, own, values, 1)
    norm_rows(x, gain, queries, inverses)
    mask = key_mask(rows, length[0])
    valid = (lax.broadcasted_iota(jnp.int32, (rows, HD), 0) < length[0]).astype(jnp.float32)

    @pl.loop(0, KV)
    def _(g):
        columns = pl.ds(pl.multiple_of(g * HD, HD), HD)
        k_group = keys[:, columns]
        v_group = values[:, columns]
        heads = group // HD
        for h in range(heads):
            place = pl.ds(pl.multiple_of(g * group + h * HD, HD), HD)
            spot = slice(h * HD, (h + 1) * HD)
            q_head = queries[:, place]
            out_grad = (valid * cotangent[:, place].astype(jnp.float32)).astype(jnp.bfloat16)
            outs[spot, :] = out_grad
            chances = chances_of(q_head, k_group, mask)
            weights[:, spot] = chances.astype(jnp.bfloat16)
            d_weight = dot(v_group, out_grad, 1, 1)
            delta = jnp.sum(chances * d_weight, axis=0, keepdims=True)
            d_score = (chances * (d_weight - delta) * scale).astype(jnp.bfloat16)
            d_scores[:, spot] = d_score
            d_queries[:, place] = dot(k_group, d_score, 0, 0).T
        q_all = jnp.concatenate(
            [queries[:, pl.ds(pl.multiple_of(g * group + h * HD, HD), HD)] for h in range(heads)], axis=0
        )
        d_value[...] = dot(weights[...], outs[...], 1, 0)
        d_key[...] = dot(d_scores[...], q_all, 1, 0)
        own_grad[0, :, columns] = d_key[prompt_count:, :]
        own_grad[1, :, columns] = d_value[prompt_count:, :]

        @pl.loop(0, table.shape[0])
        def _(j):
            target = pl.ds(pl.multiple_of(table[j] * BLOCK, BLOCK), BLOCK)
            source = pl.ds(pl.multiple_of(j * BLOCK, BLOCK), BLOCK)
            pool_grad[0, target, columns] = d_key[source, :]
            pool_grad[1, target, columns] = d_value[source, :]

    gain_grad[...] = jnp.zeros_like(gain_grad)

    @pl.loop(0, rows // BLOCK)
    def _(i):
        place = pl.ds(pl.multiple_of(i * BLOCK, BLOCK), BLOCK)
        floated = x[place, :].astype(jnp.float32)
        inverse = inverses[place, 0:1]
        d_query = d_queries[place, :]
        d_normed = d_query * gain[...]
        along = jnp.mean(d_normed * floated, axis=-1, keepdims=True)
        d_input = inverse * d_normed - floated * (inverse * inverse * inverse * along)
        input_grad[place, :] = (cotangent[place, :].astype(jnp.float32) + d_input).astype(input_grad.dtype)
        gain_grad[...] += jnp.sum(d_query * floated * inverse, axis=0, keepdims=True)


def forward(table, length, x, gain, pool, own):
    rows, width = x.shape
    count = table.shape[0] * BLOCK + rows
    vmem = pl.BlockSpec(memory_space=pltpu.VMEM)
    smem = pl.BlockSpec(memory_space=pltpu.SMEM)
    return pl.pallas_call(
        forward_kernel,
        out_shape=jax.ShapeDtypeStruct(x.shape, x.dtype),
        in_specs=[smem, smem] + [vmem] * 4,
        out_specs=vmem,
        scratch_shapes=[
            pltpu.VMEM((rows, width), jnp.bfloat16),
            pltpu.VMEM((count, pool.shape[-1]), jnp.bfloat16),
            pltpu.VMEM((count, pool.shape[-1]), jnp.bfloat16),
        ],
        compiler_params=pltpu.CompilerParams(vmem_limit_bytes=vmem_limit),
        cost_estimate=pl.CostEstimate(
            flops=4 * rows * width * count, bytes_accessed=4 * rows * width, transcendentals=rows * width // HD * count
        ),
        name="forward",
    )(table, length, x, gain, pool, own)


def backward(table, length, x, gain, pool, own, cotangent):
    rows, width = x.shape
    count = table.shape[0] * BLOCK + rows
    group = width // KV
    vmem = pl.BlockSpec(memory_space=pltpu.VMEM)
    smem = pl.BlockSpec(memory_space=pltpu.SMEM)
    return pl.pallas_call(
        backward_kernel,
        out_shape=(
            jax.ShapeDtypeStruct(x.shape, x.dtype),
            jax.ShapeDtypeStruct(pool.shape, jnp.float32),
            jax.ShapeDtypeStruct(own.shape, jnp.float32),
            jax.ShapeDtypeStruct((1, width), jnp.float32),
        ),
        in_specs=[smem, smem] + [vmem] * 5,
        out_specs=(vmem,) * 4,
        scratch_shapes=[
            pltpu.VMEM((rows, width), jnp.bfloat16),
            pltpu.VMEM((rows, HD), jnp.float32),
            pltpu.VMEM((count, pool.shape[-1]), jnp.bfloat16),
            pltpu.VMEM((count, pool.shape[-1]), jnp.bfloat16),
            pltpu.VMEM((rows * group // HD, HD), jnp.bfloat16),
            pltpu.VMEM((count, group), jnp.bfloat16),
            pltpu.VMEM((count, group), jnp.bfloat16),
            pltpu.VMEM((rows, width), jnp.float32),
            pltpu.VMEM((count, HD), jnp.float32),
            pltpu.VMEM((count, HD), jnp.float32),
        ],
        compiler_params=pltpu.CompilerParams(vmem_limit_bytes=vmem_limit),
        cost_estimate=pl.CostEstimate(
            flops=10 * rows * width * count, bytes_accessed=10 * rows * width, transcendentals=rows * width // HD * count
        ),
        name="backward",
    )(table, length, x, gain, pool, own, cotangent)


def shards(
    arriving,
    saved_input,
    returning,
    prompt_cache,
    fresh_cache,
    back_cache,
    query_gain,
    block_tables,
    fresh_lengths,
    back_lengths,
):
    cotangent = shifted_2(returning, "section", -1)
    table = block_tables[0]
    pool = lax.all_gather(prompt_cache, "fork", axis=2, tiled=True)[0]
    arriving, cotangent = lax.optimization_barrier((arriving, cotangent))
    incoming = shifted_2(arriving, "section", 1)
    input_grad, pool_grad, own_grad, gain_part = backward(
        table, back_lengths, saved_input[0, 0], query_gain, pool, back_cache[0, 0], cotangent[0, 0]
    )
    prompt_grad = lax.psum_scatter(pool_grad[None], "fork", scatter_dimension=2, tiled=True)
    gain_parts = lax.all_gather(gain_part, "fork", axis=0, tiled=True)
    section_output = forward(
        table, fresh_lengths, incoming[0, 0], query_gain, pool, fresh_cache[0, 0]
    )
    return (
        section_output[None, None],
        input_grad[None, None],
        prompt_grad,
        own_grad[None, None],
        jnp.sum(gain_parts, axis=0, keepdims=True),
    )


def solution(mesh):
    return jax.shard_map(
        shards,
        mesh=mesh,
        in_specs=(
            P("section", "fork", None, None),
            P("section", "fork", None, None),
            P("section", "fork", None, None),
            P("section", None, "fork", None),
            P("section", "fork", None, None, None),
            P("section", "fork", None, None, None),
            P("section", None),
            P("fork", None),
            P("fork"),
            P("fork"),
        ),
        out_specs=(
            P("section", "fork", None, None),
            P("section", "fork", None, None),
            P("section", None, "fork", None),
            P("section", "fork", None, None, None),
            P("section", None),
        ),
        check_vma=False,
    )
```

```python
import functools
import math

import jax
import jax.numpy as jnp
from jax import lax
from jax.experimental import pallas as pl
from jax.experimental.pallas import tpu as pltpu
from jax.sharding import PartitionSpec as P

KV = 4
HD = 128
BLOCK = 16


epsilon = 1e-06
masked_score = -1e30
scale = HD ** (-0.5)
exp_scale = scale * math.log2(math.e)
vmem_limit = 52 * 1024 * 1024


def shifted_2(value, axis, steps):
    count = lax.axis_size(axis)
    pairs = [(source, (source + steps) % count) for source in range(count)]
    return lax.ppermute(value, axis, pairs)


def gather_rows(table, pool, own, held, which):
    prompt_count = table.shape[0] * BLOCK

    @pl.loop(0, table.shape[0])
    def _(j):
        source = pl.multiple_of(table[j] * BLOCK, BLOCK)
        target = pl.multiple_of(j * BLOCK, BLOCK)
        held[pl.ds(target, BLOCK), :] = pool[which, pl.ds(source, BLOCK), :]

    held[prompt_count:, :] = own[which]


def norm_rows(x, gain, queries, inverses):
    rows = BLOCK

    @pl.loop(0, x.shape[0] // rows)
    def _(i):
        place = pl.ds(pl.multiple_of(i * rows, rows), rows)
        floated = x[place, :].astype(jnp.float32)
        inverse = lax.rsqrt(jnp.mean(floated * floated, axis=-1, keepdims=True) + epsilon)
        queries[place, :] = (floated * inverse * gain[...]).astype(jnp.bfloat16)
        if inverses is not None:
            inverses[place, :] = jnp.broadcast_to(inverse, (rows, HD))


def dot(a, b, left, right):
    return lax.dot_general(a, b, (((left,), (right,)), ((), ())), preferred_element_type=jnp.float32)


def key_mask(rows, length):
    key = lax.broadcasted_iota(jnp.int32, (rows, rows), 0)
    row = lax.broadcasted_iota(jnp.int32, (rows, rows), 1)
    return (key <= row) & (key < length)


def chances_of(q_head, keys, mask):
    rows = mask.shape[0]
    scores = dot(keys, q_head, 1, 1)
    prompt = scores[:-rows]
    recent = jnp.where(mask, scores[-rows:], masked_score)
    top = jnp.maximum(jnp.max(prompt, axis=0, keepdims=True), jnp.max(recent, axis=0, keepdims=True))
    prompt = jnp.exp2((prompt - top) * exp_scale)
    recent = jnp.exp2((recent - top) * exp_scale)
    total = jnp.sum(prompt, axis=0, keepdims=True) + jnp.sum(recent, axis=0, keepdims=True)
    return jnp.concatenate([prompt, recent], axis=0) * (1.0 / total)


def forward_kernel(table, length, x, gain, pool, own, out, queries, keys, values):
    rows, width = x.shape
    group = width // KV
    gather_rows(table, pool, own, keys, 0)
    gather_rows(table, pool, own, values, 1)
    norm_rows(x, gain, queries, None)
    mask = key_mask(rows, length[0])
    valid = (lax.broadcasted_iota(jnp.int32, (rows, HD), 0) < length[0]).astype(jnp.float32)

    @pl.loop(0, KV)
    def _(g):
        columns = pl.ds(pl.multiple_of(g * HD, HD), HD)
        k_group = keys[:, columns]
        v_group = values[:, columns]
        for h in range(group // HD):
            place = pl.ds(pl.multiple_of(g * group + h * HD, HD), HD)
            chances = chances_of(queries[:, place], k_group, mask)
            attended = dot(v_group, chances.astype(jnp.bfloat16), 0, 0).T
            out[:, place] = (x[:, place].astype(jnp.float32) + valid * attended).astype(out.dtype)


def chances_kernel(table, length, x, gain, pool, own, chances, queries, inverses, keys, values):
    rows, width = x.shape
    group = width // KV
    g = pl.program_id(0)

    @pl.when(g == 0)
    def _():
        gather_rows(table, pool, own, keys, 0)
        gather_rows(table, pool, own, values, 1)
        norm_rows(x, gain, queries, inverses)

    mask = key_mask(rows, length[0])
    k_group = keys[:, pl.ds(pl.multiple_of(g * HD, HD), HD)]
    for h in range(group // HD):
        place = pl.ds(pl.multiple_of(g * group + h * HD, HD), HD)
        chances[0, :, h * HD : (h + 1) * HD] = chances_of(queries[:, place], k_group, mask)


def backward_kernel(
    table, length, x, gain, cotangent, chances, queries, inverses, keys, values,
    input_grad, pool_grad, own_grad, gain_grad,
    outs, weights, d_scores, d_queries, d_key, d_value,
):
    rows, width = x.shape
    group = width // KV
    heads = group // HD
    prompt_count = table.shape[0] * BLOCK
    g = pl.program_id(0)

    @pl.when(g == 0)
    def _():
        pool_grad[...] = jnp.zeros_like(pool_grad)
        gain_grad[...] = jnp.zeros_like(gain_grad)

    valid = (lax.broadcasted_iota(jnp.int32, (rows, HD), 0) < length[0]).astype(jnp.float32)
    columns = pl.ds(pl.multiple_of(g * HD, HD), HD)
    k_group = keys[:, columns]
    v_group = values[:, columns]
    for h in range(heads):
        place = pl.ds(pl.multiple_of(g * group + h * HD, HD), HD)
        spot = slice(h * HD, (h + 1) * HD)
        out_grad = (valid * cotangent[:, place].astype(jnp.float32)).astype(jnp.bfloat16)
        outs[spot, :] = out_grad
        chance = chances[0, :, spot]
        weights[:, spot] = chance.astype(jnp.bfloat16)
        d_weight = dot(v_group, out_grad, 1, 1)
        delta = jnp.sum(chance * d_weight, axis=0, keepdims=True)
        d_score = (chance * (d_weight - delta) * scale).astype(jnp.bfloat16)
        d_scores[:, spot] = d_score
        d_queries[:, place] = dot(k_group, d_score, 0, 0).T
    q_all = jnp.concatenate(
        [queries[:, pl.ds(pl.multiple_of(g * group + h * HD, HD), HD)] for h in range(heads)], axis=0
    )
    d_value[...] = dot(weights[...], outs[...], 1, 0)
    d_key[...] = dot(d_scores[...], q_all, 1, 0)
    own_grad[0, :, columns] = d_key[prompt_count:, :]
    own_grad[1, :, columns] = d_value[prompt_count:, :]

    @pl.loop(0, table.shape[0])
    def _(j):
        target = pl.ds(pl.multiple_of(table[j] * BLOCK, BLOCK), BLOCK)
        source = pl.ds(pl.multiple_of(j * BLOCK, BLOCK), BLOCK)
        pool_grad[0, target, columns] = d_key[source, :]
        pool_grad[1, target, columns] = d_value[source, :]

    @pl.when(g == KV - 1)
    def _():
        @pl.loop(0, rows // BLOCK)
        def _(i):
            place = pl.ds(pl.multiple_of(i * BLOCK, BLOCK), BLOCK)
            floated = x[place, :].astype(jnp.float32)
            inverse = inverses[place, 0:1]
            d_query = d_queries[place, :]
            d_normed = d_query * gain[...]
            along = jnp.mean(d_normed * floated, axis=-1, keepdims=True)
            d_input = inverse * d_normed - floated * (inverse * inverse * inverse * along)
            input_grad[place, :] = (cotangent[place, :].astype(jnp.float32) + d_input).astype(input_grad.dtype)
            gain_grad[...] += jnp.sum(d_query * floated * inverse, axis=0, keepdims=True)


def share_kernel(
    devices, part, gain_part, prompt_grad, gain_grad,
    paired, outgoing, arrived, gain_paired, gains,
    send_a, recv_a, send_b, recv_b, send_g, recv_g, send_p, recv_p,
):
    chips = devices // 2
    rows = prompt_grad.shape[1]
    me = lax.axis_index("fork")
    chip, core = me // 2, lax.rem(me, 2)
    twin = chip * 2 + (1 - core)
    mesh_type = pl.DeviceIdType.MESH

    def slot(c, parity):
        return pl.ds(pl.multiple_of((c * 2 + parity) * rows, rows), rows)

    def after(d):
        return lax.rem(chip + d, chips)

    def pair_copy(c):
        return pltpu.make_async_remote_copy(
            src_ref=part.at[:, slot(c, 1 - core), :], dst_ref=paired.at[c],
            send_sem=send_a.at[c], recv_sem=recv_a.at[c],
            device_id={"fork": twin}, device_id_type=mesh_type,
        )

    def chip_copy(to, origin):
        return pltpu.make_async_remote_copy(
            src_ref=outgoing.at[to], dst_ref=arrived.at[origin],
            send_sem=send_b.at[to], recv_sem=recv_b.at[origin],
            device_id={"fork": to * 2 + core}, device_id_type=mesh_type,
        )

    def gain_copy(to, origin):
        return pltpu.make_async_remote_copy(
            src_ref=gains.at[chip], dst_ref=gains.at[origin],
            send_sem=send_g.at[to], recv_sem=recv_g.at[origin],
            device_id={"fork": to * 2 + core}, device_id_type=mesh_type,
        )

    gain_pair = pltpu.make_async_remote_copy(
        src_ref=gain_part, dst_ref=gain_paired, send_sem=send_p, recv_sem=recv_p,
        device_id={"fork": twin}, device_id_type=mesh_type,
    )

    barrier = pltpu.get_barrier_semaphore()
    pl.semaphore_signal(barrier, inc=1, device_id={"fork": twin}, device_id_type=mesh_type)

    @pl.loop(1, chips)
    def _(d):
        pl.semaphore_signal(
            barrier, inc=1, device_id={"fork": after(d) * 2 + core}, device_id_type=mesh_type
        )

    pl.semaphore_wait(barrier, chips)

    gain_pair.start()

    @pl.loop(1, chips + 1)
    def _(d):
        pair_copy(after(d)).start()

    gain_pair.wait()
    gains[chip] = gain_part[...] + gain_paired[...]

    @pl.loop(1, chips)
    def _(d):
        gain_copy(after(d), chip).start()

    @pl.loop(1, chips)
    def _(d):
        to = after(d)
        pair_copy(to).wait()
        outgoing[to] = (part[:, slot(to, core), :] + paired[to]).astype(outgoing.dtype)
        chip_copy(to, chip).start()

    pair_copy(chip).wait()
    prompt_grad[...] = part[:, slot(chip, core), :] + paired[chip]

    @pl.loop(1, chips)
    def _(d):
        origin = lax.rem(chip + chips - d, chips)
        gain_copy(after(d), chip).wait_send()
        gain_copy(after(d), origin).wait_recv()

    total = gains[0]
    for c in range(1, chips):
        total = total + gains[c]
    gain_grad[...] = total

    @pl.loop(1, chips)
    def _(d):
        origin = lax.rem(chip + chips - d, chips)
        chip_copy(after(d), origin).wait_recv()
        prompt_grad[...] += arrived[origin].astype(jnp.float32)

    @pl.loop(1, chips)
    def _(d):
        chip_copy(after(d), chip).wait_send()


def collect_kernel(devices, part, pool, send_a, recv_a, send_b, recv_b):
    chips = devices // 2
    rows = part.shape[1]
    me = lax.axis_index("fork")
    chip, core = me // 2, lax.rem(me, 2)
    twin = chip * 2 + (1 - core)
    mesh_type = pl.DeviceIdType.MESH

    def slot(c, parity):
        return pl.ds(pl.multiple_of((c * 2 + parity) * rows, rows), rows)

    def after(d):
        return lax.rem(chip + d, chips)

    def twin_copy(c, parity):
        return pltpu.make_async_remote_copy(
            src_ref=pool.at[:, slot(c, parity), :], dst_ref=pool.at[:, slot(c, parity), :],
            send_sem=send_a.at[c], recv_sem=recv_a.at[c],
            device_id={"fork": twin}, device_id_type=mesh_type,
        )

    def chip_copy(to, origin):
        return pltpu.make_async_remote_copy(
            src_ref=part, dst_ref=pool.at[:, slot(origin, core), :],
            send_sem=send_b.at[to], recv_sem=recv_b.at[origin],
            device_id={"fork": to * 2 + core}, device_id_type=mesh_type,
        )

    barrier = pltpu.get_barrier_semaphore()
    pl.semaphore_signal(barrier, inc=1, device_id={"fork": twin}, device_id_type=mesh_type)

    @pl.loop(1, chips)
    def _(d):
        pl.semaphore_signal(
            barrier, inc=1, device_id={"fork": after(d) * 2 + core}, device_id_type=mesh_type
        )

    pl.semaphore_wait(barrier, chips)

    @pl.loop(1, chips)
    def _(d):
        chip_copy(after(d), chip).start()

    pool[:, slot(chip, core), :] = part[...]
    twin_copy(chip, core).start()

    @pl.loop(1, chips)
    def _(d):
        origin = lax.rem(chip + chips - d, chips)
        chip_copy(after(d), origin).wait_recv()
        twin_copy(origin, core).start()

    @pl.loop(0, chips)
    def _(c):
        twin_copy(c, core).wait_send()
        twin_copy(c, 1 - core).wait_recv()

    @pl.loop(1, chips)
    def _(d):
        chip_copy(after(d), chip).wait_send()


def collect(part):
    devices = lax.axis_size("fork")
    chips = devices // 2
    kinds, rows, width = part.shape
    vmem = pl.BlockSpec(memory_space=pltpu.VMEM)
    several = pltpu.SemaphoreType.DMA((chips,))
    return pl.pallas_call(
        functools.partial(collect_kernel, devices),
        out_shape=jax.ShapeDtypeStruct((kinds, rows * devices, width), part.dtype),
        in_specs=[vmem],
        out_specs=vmem,
        scratch_shapes=[several, several, several, several],
        compiler_params=pltpu.CompilerParams(
            collective_id=1, has_side_effects=True, vmem_limit_bytes=vmem_limit
        ),
        cost_estimate=pl.CostEstimate(flops=part.size, bytes_accessed=part.size * 16, transcendentals=0),
        name="collect",
    )(part)


def share(part, gain_part):
    devices = lax.axis_size("fork")
    chips = devices // 2
    kinds, total, width = part.shape
    rows = total // devices
    vmem = pl.BlockSpec(memory_space=pltpu.VMEM)
    several = pltpu.SemaphoreType.DMA((chips,))
    single = pltpu.SemaphoreType.DMA
    return pl.pallas_call(
        functools.partial(share_kernel, devices),
        out_shape=(
            jax.ShapeDtypeStruct((kinds, rows, width), jnp.float32),
            jax.ShapeDtypeStruct(gain_part.shape, jnp.float32),
        ),
        in_specs=[vmem, vmem],
        out_specs=(vmem, vmem),
        scratch_shapes=[
            pltpu.VMEM((chips, kinds, rows, width), jnp.float32),
            pltpu.VMEM((chips, kinds, rows, width), jnp.bfloat16),
            pltpu.VMEM((chips, kinds, rows, width), jnp.bfloat16),
            pltpu.VMEM(gain_part.shape, jnp.float32),
            pltpu.VMEM((chips,) + gain_part.shape, jnp.float32),
            several, several, several, several, several, several, single, single,
        ],
        compiler_params=pltpu.CompilerParams(
            collective_id=0, has_side_effects=True, vmem_limit_bytes=vmem_limit
        ),
        cost_estimate=pl.CostEstimate(flops=part.size, bytes_accessed=part.size * 4, transcendentals=0),
        name="share",
    )(part, gain_part)


def forward(table, length, x, gain, pool, own):
    rows, width = x.shape
    count = table.shape[0] * BLOCK + rows
    vmem = pl.BlockSpec(memory_space=pltpu.VMEM)
    smem = pl.BlockSpec(memory_space=pltpu.SMEM)
    return pl.pallas_call(
        forward_kernel,
        out_shape=jax.ShapeDtypeStruct(x.shape, x.dtype),
        in_specs=[smem, smem] + [vmem] * 4,
        out_specs=vmem,
        scratch_shapes=[
            pltpu.VMEM((rows, width), jnp.bfloat16),
            pltpu.VMEM((count, pool.shape[-1]), jnp.bfloat16),
            pltpu.VMEM((count, pool.shape[-1]), jnp.bfloat16),
        ],
        compiler_params=pltpu.CompilerParams(vmem_limit_bytes=vmem_limit),
        cost_estimate=pl.CostEstimate(
            flops=4 * rows * width * count, bytes_accessed=4 * rows * width, transcendentals=rows * width // HD * count
        ),
        name="forward",
    )(table, length, x, gain, pool, own)


def whole_block(shape):
    return pl.BlockSpec(shape, lambda g: (0,) * len(shape))


def chances_call(table, length, x, gain, pool, own):
    rows, width = x.shape
    count = table.shape[0] * BLOCK + rows
    group = width // KV
    smem = pl.BlockSpec(memory_space=pltpu.SMEM)
    return pl.pallas_call(
        chances_kernel,
        grid=(KV,),
        out_shape=(
            jax.ShapeDtypeStruct((KV, count, group), jnp.float32),
            jax.ShapeDtypeStruct(x.shape, jnp.bfloat16),
            jax.ShapeDtypeStruct((rows, HD), jnp.float32),
            jax.ShapeDtypeStruct((count, pool.shape[-1]), jnp.bfloat16),
            jax.ShapeDtypeStruct((count, pool.shape[-1]), jnp.bfloat16),
        ),
        in_specs=[smem, smem] + [whole_block(v.shape) for v in (x, gain, pool, own)],
        out_specs=(
            pl.BlockSpec((1, count, group), lambda g: (g, 0, 0)),
            whole_block(x.shape),
            whole_block((rows, HD)),
            whole_block((count, pool.shape[-1])),
            whole_block((count, pool.shape[-1])),
        ),
        compiler_params=pltpu.CompilerParams(vmem_limit_bytes=vmem_limit),
        cost_estimate=pl.CostEstimate(
            flops=2 * rows * width * count, bytes_accessed=10 * rows * width, transcendentals=rows * width // HD * count
        ),
        name="chances",
    )(table, length, x, gain, pool, own)


def backward(table, length, x, gain, pool, own, cotangent, held):
    rows, width = x.shape
    count = table.shape[0] * BLOCK + rows
    group = width // KV
    smem = pl.BlockSpec(memory_space=pltpu.SMEM)
    outs = (
        jax.ShapeDtypeStruct(x.shape, x.dtype),
        jax.ShapeDtypeStruct(pool.shape, jnp.float32),
        jax.ShapeDtypeStruct(own.shape, jnp.float32),
        jax.ShapeDtypeStruct((1, width), jnp.float32),
    )
    return pl.pallas_call(
        backward_kernel,
        grid=(KV,),
        out_shape=outs,
        in_specs=[smem, smem]
        + [whole_block(v.shape) for v in (x, gain, cotangent)]
        + [pl.BlockSpec((1, count, group), lambda g: (g, 0, 0))]
        + [whole_block(v.shape) for v in held[1:]],
        out_specs=tuple(whole_block(v.shape) for v in outs),
        scratch_shapes=[
            pltpu.VMEM((rows * group // HD, HD), jnp.bfloat16),
            pltpu.VMEM((count, group), jnp.bfloat16),
            pltpu.VMEM((count, group), jnp.bfloat16),
            pltpu.VMEM((rows, width), jnp.float32),
            pltpu.VMEM((count, HD), jnp.float32),
            pltpu.VMEM((count, HD), jnp.float32),
        ],
        compiler_params=pltpu.CompilerParams(vmem_limit_bytes=vmem_limit),
        cost_estimate=pl.CostEstimate(
            flops=80 * rows * width * count, bytes_accessed=20 * rows * width, transcendentals=0
        ),
        name="backward",
    )(table, length, x, gain, cotangent, *held)


def shards(
    arriving,
    saved_input,
    returning,
    prompt_cache,
    fresh_cache,
    back_cache,
    query_gain,
    block_tables,
    fresh_lengths,
    back_lengths,
):
    cotangent = shifted_2(returning, "section", -1)
    table = block_tables[0]
    pool = collect(prompt_cache[0])
    held = chances_call(table, back_lengths, saved_input[0, 0], query_gain, pool, back_cache[0, 0])
    arriving, cotangent, inverses = lax.optimization_barrier((arriving, cotangent, held[2]))
    held = held[:2] + (inverses,) + held[3:]
    incoming = shifted_2(arriving, "section", 1)
    input_grad, pool_grad, own_grad, gain_part = backward(
        table, back_lengths, saved_input[0, 0], query_gain, pool, back_cache[0, 0], cotangent[0, 0], held
    )
    prompt_grad, gain_grad = share(pool_grad, gain_part)
    section_output = forward(
        table, fresh_lengths, incoming[0, 0], query_gain, pool, fresh_cache[0, 0]
    )
    return (
        section_output[None, None],
        input_grad[None, None],
        prompt_grad[None],
        own_grad[None, None],
        gain_grad,
    )


def solution(mesh):
    return jax.shard_map(
        shards,
        mesh=mesh,
        in_specs=(
            P("section", "fork", None, None),
            P("section", "fork", None, None),
            P("section", "fork", None, None),
            P("section", None, "fork", None),
            P("section", "fork", None, None, None),
            P("section", "fork", None, None, None),
            P("section", None),
            P("fork", None),
            P("fork"),
            P("fork"),
        ),
        out_specs=(
            P("section", "fork", None, None),
            P("section", "fork", None, None),
            P("section", None, "fork", None),
            P("section", "fork", None, None, None),
            P("section", None),
        ),
        check_vma=False,
    )
```

```python
import functools
import math

import jax
import jax.numpy as jnp
from jax import lax
from jax.experimental import pallas as pl
from jax.experimental.pallas import tpu as pltpu
from jax.sharding import PartitionSpec as P

KV = 4
HD = 128
BLOCK = 16
TOGETHER = 2


epsilon = 1e-06
masked_score = -1e30
scale = HD ** (-0.5)
exp_scale = scale * math.log2(math.e)
vmem_limit = 60 * 1024 * 1024


def shifted_2(value, axis, steps):
    count = lax.axis_size(axis)
    pairs = [(source, (source + steps) % count) for source in range(count)]
    return lax.ppermute(value, axis, pairs)


def gather_rows(table, pool, own, held, which):
    prompt_count = table.shape[0] * BLOCK

    @pl.loop(0, table.shape[0])
    def _(j):
        source = pl.multiple_of(table[j] * BLOCK, BLOCK)
        target = pl.multiple_of(j * BLOCK, BLOCK)
        held[pl.ds(target, BLOCK), :] = pool[which, pl.ds(source, BLOCK), :]

    held[prompt_count:, :] = own[which]


def norm_rows(x, gain, queries, inverses):
    rows = BLOCK

    @pl.loop(0, x.shape[0] // rows)
    def _(i):
        place = pl.ds(pl.multiple_of(i * rows, rows), rows)
        floated = x[place, :].astype(jnp.float32)
        inverse = lax.rsqrt(jnp.mean(floated * floated, axis=-1, keepdims=True) + epsilon)
        queries[place, :] = (floated * inverse * gain[...]).astype(jnp.bfloat16)
        if inverses is not None:
            inverses[place, :] = jnp.broadcast_to(inverse, (rows, HD))


def dot(a, b, left, right):
    return lax.dot_general(a, b, (((left,), (right,)), ((), ())), preferred_element_type=jnp.float32)


def key_mask(rows, length):
    key = lax.broadcasted_iota(jnp.int32, (rows, TOGETHER * rows), 0)
    row = lax.rem(lax.broadcasted_iota(jnp.int32, (rows, TOGETHER * rows), 1), rows)
    return (key <= row) & (key < length)


def head_place(g, group, h):
    return pl.ds(pl.multiple_of(g * group + h * HD, HD), HD)


def heads_of(ref, g, group, first, count):
    return jnp.concatenate([ref[:, head_place(g, group, first + k)] for k in range(count)], axis=0)


def chances_of(q_head, keys, mask):
    rows = mask.shape[0]
    scores = dot(keys, q_head, 1, 1)
    prompt = scores[:-rows]
    recent = jnp.where(mask, scores[-rows:], masked_score)
    top = jnp.maximum(jnp.max(prompt, axis=0, keepdims=True), jnp.max(recent, axis=0, keepdims=True))
    prompt = jnp.exp2((prompt - top) * exp_scale)
    recent = jnp.exp2((recent - top) * exp_scale)
    total = jnp.sum(prompt, axis=0, keepdims=True) + jnp.sum(recent, axis=0, keepdims=True)
    return jnp.concatenate([prompt, recent], axis=0) * (1.0 / total)


def forward_kernel(table, length, x, gain, pool, own, out, queries, keys, values):
    rows, width = x.shape
    group = width // KV
    gather_rows(table, pool, own, keys, 0)
    gather_rows(table, pool, own, values, 1)
    norm_rows(x, gain, queries, None)
    mask = key_mask(rows, length[0])
    valid = (lax.broadcasted_iota(jnp.int32, (rows, HD), 0) < length[0]).astype(jnp.float32)

    @pl.loop(0, KV)
    def _(g):
        columns = pl.ds(pl.multiple_of(g * HD, HD), HD)
        k_group = keys[:, columns]
        v_group = values[:, columns]
        for h in range(0, group // HD, TOGETHER):
            chances = chances_of(heads_of(queries, g, group, h, TOGETHER), k_group, mask)
            attended = dot(v_group, chances.astype(jnp.bfloat16), 0, 0).T
            for k in range(TOGETHER):
                place = head_place(g, group, h + k)
                piece = attended[k * rows : (k + 1) * rows]
                out[:, place] = (x[:, place].astype(jnp.float32) + valid * piece).astype(out.dtype)


def chances_kernel(table, length, x, gain, pool, own, chances, queries, inverses, keys, values):
    rows, width = x.shape
    group = width // KV
    g = pl.program_id(0)

    @pl.when(g == 0)
    def _():
        gather_rows(table, pool, own, keys, 0)
        gather_rows(table, pool, own, values, 1)
        norm_rows(x, gain, queries, inverses)

    mask = key_mask(rows, length[0])
    k_group = keys[:, pl.ds(pl.multiple_of(g * HD, HD), HD)]
    for h in range(0, group // HD, TOGETHER):
        chances[0, :, h * rows : (h + TOGETHER) * rows] = chances_of(
            heads_of(queries, g, group, h, TOGETHER), k_group, mask
        )


def backward_kernel(
    table, length, x, gain, cotangent, chances, queries, inverses, keys, values,
    input_grad, pool_grad, own_grad, gain_grad,
    outs, weights, d_scores, d_queries, d_key, d_value,
):
    rows, width = x.shape
    group = width // KV
    heads = group // HD
    prompt_count = table.shape[0] * BLOCK
    g = pl.program_id(0)

    @pl.when(g == 0)
    def _():
        pool_grad[...] = jnp.zeros_like(pool_grad)
        gain_grad[...] = jnp.zeros_like(gain_grad)

    row = lax.rem(lax.broadcasted_iota(jnp.int32, (TOGETHER * rows, HD), 0), rows)
    valid = (row < length[0]).astype(jnp.float32)
    columns = pl.ds(pl.multiple_of(g * HD, HD), HD)
    k_group = keys[:, columns]
    v_group = values[:, columns]
    for h in range(0, heads, TOGETHER):
        spot = slice(h * rows, (h + TOGETHER) * rows)
        out_grad = heads_of(cotangent, g, group, h, TOGETHER).astype(jnp.float32)
        out_grad = (valid * out_grad).astype(jnp.bfloat16)
        outs[spot, :] = out_grad
        chance = chances[0, :, spot]
        weights[:, spot] = chance.astype(jnp.bfloat16)
        d_weight = dot(v_group, out_grad, 1, 1)
        delta = jnp.sum(chance * d_weight, axis=0, keepdims=True)
        d_score = (chance * (d_weight - delta) * scale).astype(jnp.bfloat16)
        d_scores[:, spot] = d_score
        d_query = dot(k_group, d_score, 0, 0).T
        for k in range(TOGETHER):
            d_queries[:, head_place(g, group, h + k)] = d_query[k * rows : (k + 1) * rows]
    q_all = heads_of(queries, g, group, 0, heads)
    d_value[...] = dot(weights[...], outs[...], 1, 0)
    d_key[...] = dot(d_scores[...], q_all, 1, 0)
    own_grad[0, :, columns] = d_key[prompt_count:, :]
    own_grad[1, :, columns] = d_value[prompt_count:, :]

    @pl.loop(0, table.shape[0])
    def _(j):
        target = pl.ds(pl.multiple_of(table[j] * BLOCK, BLOCK), BLOCK)
        source = pl.ds(pl.multiple_of(j * BLOCK, BLOCK), BLOCK)
        pool_grad[0, target, columns] = d_key[source, :]
        pool_grad[1, target, columns] = d_value[source, :]

    @pl.when(g == KV - 1)
    def _():
        @pl.loop(0, rows // BLOCK)
        def _(i):
            place = pl.ds(pl.multiple_of(i * BLOCK, BLOCK), BLOCK)
            floated = x[place, :].astype(jnp.float32)
            inverse = inverses[place, 0:1]
            d_query = d_queries[place, :]
            d_normed = d_query * gain[...]
            along = jnp.mean(d_normed * floated, axis=-1, keepdims=True)
            d_input = inverse * d_normed - floated * (inverse * inverse * inverse * along)
            input_grad[place, :] = (cotangent[place, :].astype(jnp.float32) + d_input).astype(input_grad.dtype)
            gain_grad[...] += jnp.sum(d_query * floated * inverse, axis=0, keepdims=True)


def share_kernel(
    devices, part, gain_part, prompt_grad, gain_grad,
    paired, outgoing, arrived, gain_paired, gains,
    send_a, recv_a, send_b, recv_b, send_g, recv_g, send_p, recv_p,
):
    chips = devices // 2
    rows = prompt_grad.shape[1]
    me = lax.axis_index("fork")
    chip, core = me // 2, lax.rem(me, 2)
    twin = chip * 2 + (1 - core)
    mesh_type = pl.DeviceIdType.MESH

    def slot(c, parity):
        return pl.ds(pl.multiple_of((c * 2 + parity) * rows, rows), rows)

    def after(d):
        return lax.rem(chip + d, chips)

    def pair_copy(c):
        return pltpu.make_async_remote_copy(
            src_ref=part.at[:, slot(c, 1 - core), :], dst_ref=paired.at[c],
            send_sem=send_a.at[c], recv_sem=recv_a.at[c],
            device_id={"fork": twin}, device_id_type=mesh_type,
        )

    def chip_copy(to, origin):
        return pltpu.make_async_remote_copy(
            src_ref=outgoing.at[to], dst_ref=arrived.at[origin],
            send_sem=send_b.at[to], recv_sem=recv_b.at[origin],
            device_id={"fork": to * 2 + core}, device_id_type=mesh_type,
        )

    def gain_copy(to, origin):
        return pltpu.make_async_remote_copy(
            src_ref=gains.at[chip], dst_ref=gains.at[origin],
            send_sem=send_g.at[to], recv_sem=recv_g.at[origin],
            device_id={"fork": to * 2 + core}, device_id_type=mesh_type,
        )

    gain_pair = pltpu.make_async_remote_copy(
        src_ref=gain_part, dst_ref=gain_paired, send_sem=send_p, recv_sem=recv_p,
        device_id={"fork": twin}, device_id_type=mesh_type,
    )

    barrier = pltpu.get_barrier_semaphore()
    pl.semaphore_signal(barrier, inc=1, device_id={"fork": twin}, device_id_type=mesh_type)

    @pl.loop(1, chips)
    def _(d):
        pl.semaphore_signal(
            barrier, inc=1, device_id={"fork": after(d) * 2 + core}, device_id_type=mesh_type
        )

    pl.semaphore_wait(barrier, chips)

    gain_pair.start()

    @pl.loop(1, chips + 1)
    def _(d):
        pair_copy(after(d)).start()

    gain_pair.wait()
    gains[chip] = gain_part[...] + gain_paired[...]

    @pl.loop(1, chips)
    def _(d):
        gain_copy(after(d), chip).start()

    @pl.loop(1, chips)
    def _(d):
        to = after(d)
        pair_copy(to).wait()
        outgoing[to] = (part[:, slot(to, core), :] + paired[to]).astype(outgoing.dtype)
        chip_copy(to, chip).start()

    pair_copy(chip).wait()
    prompt_grad[...] = part[:, slot(chip, core), :] + paired[chip]

    @pl.loop(1, chips)
    def _(d):
        origin = lax.rem(chip + chips - d, chips)
        gain_copy(after(d), chip).wait_send()
        gain_copy(after(d), origin).wait_recv()

    total = gains[0]
    for c in range(1, chips):
        total = total + gains[c]
    gain_grad[...] = total

    @pl.loop(1, chips)
    def _(d):
        origin = lax.rem(chip + chips - d, chips)
        chip_copy(after(d), origin).wait_recv()
        prompt_grad[...] += arrived[origin].astype(jnp.float32)

    @pl.loop(1, chips)
    def _(d):
        chip_copy(after(d), chip).wait_send()


def collect_kernel(devices, part, pool, send_a, recv_a, send_b, recv_b):
    chips = devices // 2
    rows = part.shape[1]
    me = lax.axis_index("fork")
    chip, core = me // 2, lax.rem(me, 2)
    twin = chip * 2 + (1 - core)
    mesh_type = pl.DeviceIdType.MESH

    def slot(c, parity):
        return pl.ds(pl.multiple_of((c * 2 + parity) * rows, rows), rows)

    def after(d):
        return lax.rem(chip + d, chips)

    def twin_copy(c, parity):
        return pltpu.make_async_remote_copy(
            src_ref=pool.at[:, slot(c, parity), :], dst_ref=pool.at[:, slot(c, parity), :],
            send_sem=send_a.at[c], recv_sem=recv_a.at[c],
            device_id={"fork": twin}, device_id_type=mesh_type,
        )

    def chip_copy(to, origin):
        return pltpu.make_async_remote_copy(
            src_ref=part, dst_ref=pool.at[:, slot(origin, core), :],
            send_sem=send_b.at[to], recv_sem=recv_b.at[origin],
            device_id={"fork": to * 2 + core}, device_id_type=mesh_type,
        )

    barrier = pltpu.get_barrier_semaphore()
    pl.semaphore_signal(barrier, inc=1, device_id={"fork": twin}, device_id_type=mesh_type)

    @pl.loop(1, chips)
    def _(d):
        pl.semaphore_signal(
            barrier, inc=1, device_id={"fork": after(d) * 2 + core}, device_id_type=mesh_type
        )

    pl.semaphore_wait(barrier, chips)

    @pl.loop(1, chips)
    def _(d):
        chip_copy(after(d), chip).start()

    pool[:, slot(chip, core), :] = part[...]
    twin_copy(chip, core).start()

    @pl.loop(1, chips)
    def _(d):
        origin = lax.rem(chip + chips - d, chips)
        chip_copy(after(d), origin).wait_recv()
        twin_copy(origin, core).start()

    @pl.loop(0, chips)
    def _(c):
        twin_copy(c, core).wait_send()
        twin_copy(c, 1 - core).wait_recv()

    @pl.loop(1, chips)
    def _(d):
        chip_copy(after(d), chip).wait_send()


def collect(part):
    devices = lax.axis_size("fork")
    chips = devices // 2
    kinds, rows, width = part.shape
    vmem = pl.BlockSpec(memory_space=pltpu.VMEM)
    several = pltpu.SemaphoreType.DMA((chips,))
    return pl.pallas_call(
        functools.partial(collect_kernel, devices),
        out_shape=jax.ShapeDtypeStruct((kinds, rows * devices, width), part.dtype),
        in_specs=[vmem],
        out_specs=vmem,
        scratch_shapes=[several, several, several, several],
        compiler_params=pltpu.CompilerParams(
            collective_id=1, has_side_effects=True, vmem_limit_bytes=vmem_limit
        ),
        cost_estimate=pl.CostEstimate(flops=part.size, bytes_accessed=part.size * 16, transcendentals=0),
        name="collect",
    )(part)


def share(part, gain_part):
    devices = lax.axis_size("fork")
    chips = devices // 2
    kinds, total, width = part.shape
    rows = total // devices
    vmem = pl.BlockSpec(memory_space=pltpu.VMEM)
    several = pltpu.SemaphoreType.DMA((chips,))
    single = pltpu.SemaphoreType.DMA
    return pl.pallas_call(
        functools.partial(share_kernel, devices),
        out_shape=(
            jax.ShapeDtypeStruct((kinds, rows, width), jnp.float32),
            jax.ShapeDtypeStruct(gain_part.shape, jnp.float32),
        ),
        in_specs=[vmem, vmem],
        out_specs=(vmem, vmem),
        scratch_shapes=[
            pltpu.VMEM((chips, kinds, rows, width), jnp.float32),
            pltpu.VMEM((chips, kinds, rows, width), jnp.bfloat16),
            pltpu.VMEM((chips, kinds, rows, width), jnp.bfloat16),
            pltpu.VMEM(gain_part.shape, jnp.float32),
            pltpu.VMEM((chips,) + gain_part.shape, jnp.float32),
            several, several, several, several, several, several, single, single,
        ],
        compiler_params=pltpu.CompilerParams(
            collective_id=0, has_side_effects=True, vmem_limit_bytes=vmem_limit
        ),
        cost_estimate=pl.CostEstimate(flops=part.size, bytes_accessed=part.size * 4, transcendentals=0),
        name="share",
    )(part, gain_part)


def forward(table, length, x, gain, pool, own):
    rows, width = x.shape
    count = table.shape[0] * BLOCK + rows
    vmem = pl.BlockSpec(memory_space=pltpu.VMEM)
    smem = pl.BlockSpec(memory_space=pltpu.SMEM)
    return pl.pallas_call(
        forward_kernel,
        out_shape=jax.ShapeDtypeStruct(x.shape, x.dtype),
        in_specs=[smem, smem] + [vmem] * 4,
        out_specs=vmem,
        scratch_shapes=[
            pltpu.VMEM((rows, width), jnp.bfloat16),
            pltpu.VMEM((count, pool.shape[-1]), jnp.bfloat16),
            pltpu.VMEM((count, pool.shape[-1]), jnp.bfloat16),
        ],
        compiler_params=pltpu.CompilerParams(vmem_limit_bytes=vmem_limit),
        cost_estimate=pl.CostEstimate(
            flops=4 * rows * width * count, bytes_accessed=4 * rows * width, transcendentals=rows * width // HD * count
        ),
        name="forward",
    )(table, length, x, gain, pool, own)


def whole_block(shape):
    return pl.BlockSpec(shape, lambda g: (0,) * len(shape))


def chances_call(table, length, x, gain, pool, own):
    rows, width = x.shape
    count = table.shape[0] * BLOCK + rows
    group = width // KV
    smem = pl.BlockSpec(memory_space=pltpu.SMEM)
    return pl.pallas_call(
        chances_kernel,
        grid=(KV,),
        out_shape=(
            jax.ShapeDtypeStruct((KV, count, group // HD * rows), jnp.float32),
            jax.ShapeDtypeStruct(x.shape, jnp.bfloat16),
            jax.ShapeDtypeStruct((rows, HD), jnp.float32),
            jax.ShapeDtypeStruct((count, pool.shape[-1]), jnp.bfloat16),
            jax.ShapeDtypeStruct((count, pool.shape[-1]), jnp.bfloat16),
        ),
        in_specs=[smem, smem] + [whole_block(v.shape) for v in (x, gain, pool, own)],
        out_specs=(
            pl.BlockSpec((1, count, group // HD * rows), lambda g: (g, 0, 0)),
            whole_block(x.shape),
            whole_block((rows, HD)),
            whole_block((count, pool.shape[-1])),
            whole_block((count, pool.shape[-1])),
        ),
        compiler_params=pltpu.CompilerParams(vmem_limit_bytes=vmem_limit),
        cost_estimate=pl.CostEstimate(
            flops=2 * rows * width * count, bytes_accessed=10 * rows * width, transcendentals=rows * width // HD * count
        ),
        name="chances",
    )(table, length, x, gain, pool, own)


def backward(table, length, x, gain, pool, own, cotangent, held):
    rows, width = x.shape
    count = table.shape[0] * BLOCK + rows
    group = width // KV
    smem = pl.BlockSpec(memory_space=pltpu.SMEM)
    outs = (
        jax.ShapeDtypeStruct(x.shape, x.dtype),
        jax.ShapeDtypeStruct(pool.shape, jnp.float32),
        jax.ShapeDtypeStruct(own.shape, jnp.float32),
        jax.ShapeDtypeStruct((1, width), jnp.float32),
    )
    return pl.pallas_call(
        backward_kernel,
        grid=(KV,),
        out_shape=outs,
        in_specs=[smem, smem]
        + [whole_block(v.shape) for v in (x, gain, cotangent)]
        + [pl.BlockSpec((1, count, group // HD * rows), lambda g: (g, 0, 0))]
        + [whole_block(v.shape) for v in held[1:]],
        out_specs=tuple(whole_block(v.shape) for v in outs),
        scratch_shapes=[
            pltpu.VMEM((rows * group // HD, HD), jnp.bfloat16),
            pltpu.VMEM((count, group // HD * rows), jnp.bfloat16),
            pltpu.VMEM((count, group // HD * rows), jnp.bfloat16),
            pltpu.VMEM((rows, width), jnp.float32),
            pltpu.VMEM((count, HD), jnp.float32),
            pltpu.VMEM((count, HD), jnp.float32),
        ],
        compiler_params=pltpu.CompilerParams(vmem_limit_bytes=vmem_limit),
        cost_estimate=pl.CostEstimate(
            flops=80 * rows * width * count, bytes_accessed=20 * rows * width, transcendentals=0
        ),
        name="backward",
    )(table, length, x, gain, cotangent, *held)


def shards(
    arriving,
    saved_input,
    returning,
    prompt_cache,
    fresh_cache,
    back_cache,
    query_gain,
    block_tables,
    fresh_lengths,
    back_lengths,
):
    cotangent = shifted_2(returning, "section", -1)
    table = block_tables[0]
    pool = collect(prompt_cache[0])
    held = chances_call(table, back_lengths, saved_input[0, 0], query_gain, pool, back_cache[0, 0])
    arriving, cotangent, inverses = lax.optimization_barrier((arriving, cotangent, held[2]))
    held = held[:2] + (inverses,) + held[3:]
    incoming = shifted_2(arriving, "section", 1)
    input_grad, pool_grad, own_grad, gain_part = backward(
        table, back_lengths, saved_input[0, 0], query_gain, pool, back_cache[0, 0], cotangent[0, 0], held
    )
    prompt_grad, gain_grad = share(pool_grad, gain_part)
    section_output = forward(
        table, fresh_lengths, incoming[0, 0], query_gain, pool, fresh_cache[0, 0]
    )
    return (
        section_output[None, None],
        input_grad[None, None],
        prompt_grad[None],
        own_grad[None, None],
        gain_grad,
    )


def solution(mesh):
    return jax.shard_map(
        shards,
        mesh=mesh,
        in_specs=(
            P("section", "fork", None, None),
            P("section", "fork", None, None),
            P("section", "fork", None, None),
            P("section", None, "fork", None),
            P("section", "fork", None, None, None),
            P("section", "fork", None, None, None),
            P("section", None),
            P("fork", None),
            P("fork"),
            P("fork"),
        ),
        out_specs=(
            P("section", "fork", None, None),
            P("section", "fork", None, None),
            P("section", None, "fork", None),
            P("section", "fork", None, None, None),
            P("section", None),
        ),
        check_vma=False,
    )
```

```python
import functools
import math

import jax
import jax.numpy as jnp
from jax import lax
from jax.experimental import pallas as pl
from jax.experimental.pallas import tpu as pltpu
from jax.sharding import PartitionSpec as P

KV = 4
HD = 128
BLOCK = 16
TOGETHER = 2


epsilon = 1e-06
masked_score = -1e30
scale = HD ** (-0.5)
exp_scale = scale * math.log2(math.e)
vmem_limit = 52 * 1024 * 1024
back_limit = 56 * 1024 * 1024
wide_limit = 60 * 1024 * 1024


def shifted_2(value, axis, steps):
    count = lax.axis_size(axis)
    pairs = [(source, (source + steps) % count) for source in range(count)]
    return lax.ppermute(value, axis, pairs)


def gather_rows(table, pool, own, held, which):
    prompt_count = table.shape[0] * BLOCK

    @pl.loop(0, table.shape[0])
    def _(j):
        source = pl.multiple_of(table[j] * BLOCK, BLOCK)
        target = pl.multiple_of(j * BLOCK, BLOCK)
        held[pl.ds(target, BLOCK), :] = pool[which, pl.ds(source, BLOCK), :]

    held[prompt_count:, :] = own[which]


def norm_rows(x, gain, queries, inverses):
    rows = BLOCK

    @pl.loop(0, x.shape[0] // rows)
    def _(i):
        place = pl.ds(pl.multiple_of(i * rows, rows), rows)
        floated = x[place, :].astype(jnp.float32)
        inverse = lax.rsqrt(jnp.mean(floated * floated, axis=-1, keepdims=True) + epsilon)
        queries[place, :] = (floated * inverse * gain[...]).astype(jnp.bfloat16)
        if inverses is not None:
            inverses[place, :] = jnp.broadcast_to(inverse, (rows, HD))


def dot(a, b, left, right):
    return lax.dot_general(a, b, (((left,), (right,)), ((), ())), preferred_element_type=jnp.float32)


def key_mask(rows, length):
    key = lax.broadcasted_iota(jnp.int32, (rows, TOGETHER * rows), 0)
    row = lax.rem(lax.broadcasted_iota(jnp.int32, (rows, TOGETHER * rows), 1), rows)
    return (key <= row) & (key < length)


def head_place(g, group, h):
    return pl.ds(pl.multiple_of(g * group + h * HD, HD), HD)


def heads_of(ref, g, group, first, count):
    return jnp.concatenate([ref[:, head_place(g, group, first + k)] for k in range(count)], axis=0)


def chances_of(q_head, keys, mask):
    rows = mask.shape[0]
    scores = dot(keys, q_head, 1, 1)
    prompt = scores[:-rows]
    recent = jnp.where(mask, scores[-rows:], masked_score)
    top = jnp.maximum(jnp.max(prompt, axis=0, keepdims=True), jnp.max(recent, axis=0, keepdims=True))
    prompt = jnp.exp2((prompt - top) * exp_scale)
    recent = jnp.exp2((recent - top) * exp_scale)
    total = jnp.sum(prompt, axis=0, keepdims=True) + jnp.sum(recent, axis=0, keepdims=True)
    return jnp.concatenate([prompt, recent], axis=0) * (1.0 / total)


def forward_kernel(table, length, x, gain, pool, own, out, queries, keys, values):
    rows, width = x.shape
    group = width // KV
    g = pl.program_id(0)

    @pl.when(g == 0)
    def _():
        gather_rows(table, pool, own, keys, 0)
        gather_rows(table, pool, own, values, 1)
        norm_rows(x, gain, queries, None)

    mask = key_mask(rows, length[0])
    valid = (lax.broadcasted_iota(jnp.int32, (rows, HD), 0) < length[0]).astype(jnp.float32)
    columns = pl.ds(pl.multiple_of(g * HD, HD), HD)
    k_group = keys[:, columns]
    v_group = values[:, columns]
    for h in range(0, group // HD, TOGETHER):
        chances = chances_of(heads_of(queries, g, group, h, TOGETHER), k_group, mask)
        attended = dot(v_group, chances.astype(jnp.bfloat16), 0, 0).T
        for k in range(TOGETHER):
            floated = x[:, head_place(g, group, h + k)].astype(jnp.float32)
            piece = attended[k * rows : (k + 1) * rows]
            out[:, (h + k) * HD : (h + k + 1) * HD] = (floated + valid * piece).astype(out.dtype)


def chances_kernel(table, length, x, gain, pool, own, chances, queries, inverses, keys, values):
    rows, width = x.shape
    group = width // KV
    g = pl.program_id(0)

    @pl.when(g == 0)
    def _():
        gather_rows(table, pool, own, keys, 0)
        gather_rows(table, pool, own, values, 1)
        norm_rows(x, gain, queries, inverses)

    mask = key_mask(rows, length[0])
    k_group = keys[:, pl.ds(pl.multiple_of(g * HD, HD), HD)]
    for h in range(0, group // HD, TOGETHER):
        chances[0, :, h * rows : (h + TOGETHER) * rows] = chances_of(
            heads_of(queries, g, group, h, TOGETHER), k_group, mask
        )


def backward_kernel(
    table, length, x, gain, cotangent, chances, queries, inverses, keys, values,
    input_grad, pool_grad, own_grad, gain_grad,
    outs, weights, d_scores, d_queries, d_key, d_value,
):
    rows, width = x.shape
    group = width // KV
    heads = group // HD
    prompt_count = table.shape[0] * BLOCK
    g = pl.program_id(0)

    @pl.when(g == 0)
    def _():
        pool_grad[...] = jnp.zeros_like(pool_grad)
        gain_grad[...] = jnp.zeros_like(gain_grad)

    row = lax.rem(lax.broadcasted_iota(jnp.int32, (TOGETHER * rows, HD), 0), rows)
    valid = (row < length[0]).astype(jnp.float32)
    columns = pl.ds(pl.multiple_of(g * HD, HD), HD)
    k_group = keys[:, columns]
    v_group = values[:, columns]
    for h in range(0, heads, TOGETHER):
        spot = slice(h * rows, (h + TOGETHER) * rows)
        out_grad = heads_of(cotangent, g, group, h, TOGETHER).astype(jnp.float32)
        out_grad = (valid * out_grad).astype(jnp.bfloat16)
        outs[spot, :] = out_grad
        chance = chances[0, :, spot]
        weights[:, spot] = chance.astype(jnp.bfloat16)
        d_weight = dot(v_group, out_grad, 1, 1)
        delta = jnp.sum(chance * d_weight, axis=0, keepdims=True)
        d_score = (chance * (d_weight - delta) * scale).astype(jnp.bfloat16)
        d_scores[:, spot] = d_score
        d_query = dot(k_group, d_score, 0, 0).T
        for k in range(TOGETHER):
            d_queries[:, head_place(g, group, h + k)] = d_query[k * rows : (k + 1) * rows]
    q_all = heads_of(queries, g, group, 0, heads)
    d_value[...] = dot(weights[...], outs[...], 1, 0)
    d_key[...] = dot(d_scores[...], q_all, 1, 0)
    own_grad[0, :, columns] = d_key[prompt_count:, :]
    own_grad[1, :, columns] = d_value[prompt_count:, :]

    @pl.loop(0, table.shape[0])
    def _(j):
        target = pl.ds(pl.multiple_of(table[j] * BLOCK, BLOCK), BLOCK)
        source = pl.ds(pl.multiple_of(j * BLOCK, BLOCK), BLOCK)
        pool_grad[0, target, columns] = d_key[source, :]
        pool_grad[1, target, columns] = d_value[source, :]

    @pl.when(g == KV - 1)
    def _():
        @pl.loop(0, rows // BLOCK)
        def _(i):
            place = pl.ds(pl.multiple_of(i * BLOCK, BLOCK), BLOCK)
            floated = x[place, :].astype(jnp.float32)
            inverse = inverses[place, 0:1]
            d_query = d_queries[place, :]
            d_normed = d_query * gain[...]
            along = jnp.mean(d_normed * floated, axis=-1, keepdims=True)
            d_input = inverse * d_normed - floated * (inverse * inverse * inverse * along)
            input_grad[place, :] = (cotangent[place, :].astype(jnp.float32) + d_input).astype(input_grad.dtype)
            gain_grad[...] += jnp.sum(d_query * floated * inverse, axis=0, keepdims=True)


def share_kernel(
    devices, part, gain_part, prompt_grad, gain_grad,
    paired, outgoing, arrived, gain_paired, gains,
    send_a, recv_a, send_b, recv_b, send_g, recv_g, send_p, recv_p,
):
    chips = devices // 2
    rows = prompt_grad.shape[1]
    me = lax.axis_index("fork")
    chip, core = me // 2, lax.rem(me, 2)
    twin = chip * 2 + (1 - core)
    mesh_type = pl.DeviceIdType.MESH

    def slot(c, parity):
        return pl.ds(pl.multiple_of((c * 2 + parity) * rows, rows), rows)

    def after(d):
        return lax.rem(chip + d, chips)

    def far(d):
        return after(1 + lax.rem(chips // 2 + d - 2, chips - 1))

    def pair_copy(c):
        return pltpu.make_async_remote_copy(
            src_ref=part.at[:, slot(c, 1 - core), :], dst_ref=paired.at[c],
            send_sem=send_a.at[c], recv_sem=recv_a.at[c],
            device_id={"fork": twin}, device_id_type=mesh_type,
        )

    def chip_copy(to, origin):
        return pltpu.make_async_remote_copy(
            src_ref=outgoing.at[to], dst_ref=arrived.at[origin],
            send_sem=send_b.at[to], recv_sem=recv_b.at[origin],
            device_id={"fork": to * 2 + core}, device_id_type=mesh_type,
        )

    def gain_copy(to, origin):
        return pltpu.make_async_remote_copy(
            src_ref=gains.at[chip], dst_ref=gains.at[origin],
            send_sem=send_g.at[to], recv_sem=recv_g.at[origin],
            device_id={"fork": to * 2 + core}, device_id_type=mesh_type,
        )

    gain_pair = pltpu.make_async_remote_copy(
        src_ref=gain_part, dst_ref=gain_paired, send_sem=send_p, recv_sem=recv_p,
        device_id={"fork": twin}, device_id_type=mesh_type,
    )

    barrier = pltpu.get_barrier_semaphore()
    pl.semaphore_signal(barrier, inc=1, device_id={"fork": twin}, device_id_type=mesh_type)

    @pl.loop(1, chips)
    def _(d):
        pl.semaphore_signal(
            barrier, inc=1, device_id={"fork": after(d) * 2 + core}, device_id_type=mesh_type
        )

    pl.semaphore_wait(barrier, chips)

    gain_pair.start()

    @pl.loop(1, chips)
    def _(d):
        pair_copy(far(d)).start()

    pair_copy(chip).start()

    gain_pair.wait()
    gains[chip] = gain_part[...] + gain_paired[...]

    @pl.loop(1, chips)
    def _(d):
        gain_copy(after(d), chip).start()

    @pl.loop(1, chips)
    def _(d):
        to = far(d)
        pair_copy(to).wait()
        outgoing[to] = (part[:, slot(to, core), :] + paired[to]).astype(outgoing.dtype)
        chip_copy(to, chip).start()

    pair_copy(chip).wait()
    prompt_grad[...] = part[:, slot(chip, core), :] + paired[chip]

    @pl.loop(1, chips)
    def _(d):
        origin = lax.rem(chip + chips - d, chips)
        gain_copy(after(d), chip).wait_send()
        gain_copy(after(d), origin).wait_recv()

    total = gains[0]
    for c in range(1, chips):
        total = total + gains[c]
    gain_grad[...] = total

    @pl.loop(1, chips)
    def _(d):
        origin = lax.rem(chip + chips - d, chips)
        chip_copy(after(d), origin).wait_recv()
        prompt_grad[...] += arrived[origin].astype(jnp.float32)

    @pl.loop(1, chips)
    def _(d):
        chip_copy(after(d), chip).wait_send()


def collect_kernel(devices, part, pool, send_a, recv_a, send_b, recv_b):
    chips = devices // 2
    rows = part.shape[1]
    me = lax.axis_index("fork")
    chip, core = me // 2, lax.rem(me, 2)
    twin = chip * 2 + (1 - core)
    mesh_type = pl.DeviceIdType.MESH

    def slot(c, parity):
        return pl.ds(pl.multiple_of((c * 2 + parity) * rows, rows), rows)

    def after(d):
        return lax.rem(chip + d, chips)

    def far(d):
        return after(1 + lax.rem(chips // 2 + d - 2, chips - 1))

    def twin_copy(c, parity):
        return pltpu.make_async_remote_copy(
            src_ref=pool.at[:, slot(c, parity), :], dst_ref=pool.at[:, slot(c, parity), :],
            send_sem=send_a.at[c], recv_sem=recv_a.at[c],
            device_id={"fork": twin}, device_id_type=mesh_type,
        )

    def chip_copy(to, origin):
        return pltpu.make_async_remote_copy(
            src_ref=part, dst_ref=pool.at[:, slot(origin, core), :],
            send_sem=send_b.at[to], recv_sem=recv_b.at[origin],
            device_id={"fork": to * 2 + core}, device_id_type=mesh_type,
        )

    barrier = pltpu.get_barrier_semaphore()
    pl.semaphore_signal(barrier, inc=1, device_id={"fork": twin}, device_id_type=mesh_type)

    @pl.loop(1, chips)
    def _(d):
        pl.semaphore_signal(
            barrier, inc=1, device_id={"fork": after(d) * 2 + core}, device_id_type=mesh_type
        )

    pl.semaphore_wait(barrier, chips)

    @pl.loop(1, chips)
    def _(d):
        chip_copy(far(d), chip).start()

    pool[:, slot(chip, core), :] = part[...]
    twin_copy(chip, core).start()

    @pl.loop(1, chips)
    def _(d):
        origin = lax.rem(chip + chips - d, chips)
        chip_copy(after(d), origin).wait_recv()
        twin_copy(origin, core).start()

    @pl.loop(0, chips)
    def _(c):
        twin_copy(c, core).wait_send()
        twin_copy(c, 1 - core).wait_recv()

    @pl.loop(1, chips)
    def _(d):
        chip_copy(after(d), chip).wait_send()


def collect(part):
    devices = lax.axis_size("fork")
    chips = devices // 2
    kinds, rows, width = part.shape
    vmem = pl.BlockSpec(memory_space=pltpu.VMEM)
    several = pltpu.SemaphoreType.DMA((chips,))
    return pl.pallas_call(
        functools.partial(collect_kernel, devices),
        out_shape=jax.ShapeDtypeStruct((kinds, rows * devices, width), part.dtype),
        in_specs=[vmem],
        out_specs=vmem,
        scratch_shapes=[several, several, several, several],
        compiler_params=pltpu.CompilerParams(
            collective_id=1, has_side_effects=True, vmem_limit_bytes=vmem_limit
        ),
        cost_estimate=pl.CostEstimate(flops=part.size, bytes_accessed=part.size * 16, transcendentals=0),
        name="collect",
    )(part)


def share(part, gain_part):
    devices = lax.axis_size("fork")
    chips = devices // 2
    kinds, total, width = part.shape
    rows = total // devices
    vmem = pl.BlockSpec(memory_space=pltpu.VMEM)
    several = pltpu.SemaphoreType.DMA((chips,))
    single = pltpu.SemaphoreType.DMA
    return pl.pallas_call(
        functools.partial(share_kernel, devices),
        out_shape=(
            jax.ShapeDtypeStruct((kinds, rows, width), jnp.float32),
            jax.ShapeDtypeStruct(gain_part.shape, jnp.float32),
        ),
        in_specs=[vmem, vmem],
        out_specs=(vmem, vmem),
        scratch_shapes=[
            pltpu.VMEM((chips, kinds, rows, width), jnp.float32),
            pltpu.VMEM((chips, kinds, rows, width), jnp.bfloat16),
            pltpu.VMEM((chips, kinds, rows, width), jnp.bfloat16),
            pltpu.VMEM(gain_part.shape, jnp.float32),
            pltpu.VMEM((chips,) + gain_part.shape, jnp.float32),
            several, several, several, several, several, several, single, single,
        ],
        compiler_params=pltpu.CompilerParams(
            collective_id=0, has_side_effects=True, vmem_limit_bytes=vmem_limit
        ),
        cost_estimate=pl.CostEstimate(flops=part.size, bytes_accessed=part.size * 4, transcendentals=0),
        name="share",
    )(part, gain_part)


def forward(table, length, x, gain, pool, own):
    rows, width = x.shape
    count = table.shape[0] * BLOCK + rows
    group = width // KV
    smem = pl.BlockSpec(memory_space=pltpu.SMEM)
    return pl.pallas_call(
        forward_kernel,
        grid=(KV,),
        out_shape=jax.ShapeDtypeStruct(x.shape, x.dtype),
        in_specs=[smem, smem] + [whole_block(v.shape) for v in (x, gain, pool, own)],
        out_specs=pl.BlockSpec((rows, group), lambda g: (0, g)),
        scratch_shapes=[
            pltpu.VMEM((rows, width), jnp.bfloat16),
            pltpu.VMEM((count, pool.shape[-1]), jnp.bfloat16),
            pltpu.VMEM((count, pool.shape[-1]), jnp.bfloat16),
        ],
        compiler_params=pltpu.CompilerParams(vmem_limit_bytes=vmem_limit),
        cost_estimate=pl.CostEstimate(
            flops=4 * rows * width * count, bytes_accessed=4 * rows * width, transcendentals=rows * width // HD * count
        ),
        name="forward",
    )(table, length, x, gain, pool, own)


def whole_block(shape):
    return pl.BlockSpec(shape, lambda g: (0,) * len(shape))


def chances_call(table, length, x, gain, pool, own):
    rows, width = x.shape
    count = table.shape[0] * BLOCK + rows
    group = width // KV
    smem = pl.BlockSpec(memory_space=pltpu.SMEM)
    return pl.pallas_call(
        chances_kernel,
        grid=(KV,),
        out_shape=(
            jax.ShapeDtypeStruct((KV, count, group // HD * rows), jnp.float32),
            jax.ShapeDtypeStruct(x.shape, jnp.bfloat16),
            jax.ShapeDtypeStruct((rows, HD), jnp.float32),
            jax.ShapeDtypeStruct((count, pool.shape[-1]), jnp.bfloat16),
            jax.ShapeDtypeStruct((count, pool.shape[-1]), jnp.bfloat16),
        ),
        in_specs=[smem, smem] + [whole_block(v.shape) for v in (x, gain, pool, own)],
        out_specs=(
            pl.BlockSpec((1, count, group // HD * rows), lambda g: (g, 0, 0)),
            whole_block(x.shape),
            whole_block((rows, HD)),
            whole_block((count, pool.shape[-1])),
            whole_block((count, pool.shape[-1])),
        ),
        compiler_params=pltpu.CompilerParams(vmem_limit_bytes=wide_limit),
        cost_estimate=pl.CostEstimate(
            flops=2 * rows * width * count, bytes_accessed=10 * rows * width, transcendentals=rows * width // HD * count
        ),
        name="chances",
    )(table, length, x, gain, pool, own)


def backward(table, length, x, gain, pool, own, cotangent, held):
    rows, width = x.shape
    count = table.shape[0] * BLOCK + rows
    group = width // KV
    smem = pl.BlockSpec(memory_space=pltpu.SMEM)
    outs = (
        jax.ShapeDtypeStruct(x.shape, x.dtype),
        jax.ShapeDtypeStruct(pool.shape, jnp.float32),
        jax.ShapeDtypeStruct(own.shape, jnp.float32),
        jax.ShapeDtypeStruct((1, width), jnp.float32),
    )
    return pl.pallas_call(
        backward_kernel,
        grid=(KV,),
        out_shape=outs,
        in_specs=[smem, smem]
        + [whole_block(v.shape) for v in (x, gain, cotangent)]
        + [pl.BlockSpec((1, count, group // HD * rows), lambda g: (g, 0, 0))]
        + [whole_block(v.shape) for v in held[1:]],
        out_specs=tuple(whole_block(v.shape) for v in outs),
        scratch_shapes=[
            pltpu.VMEM((rows * group // HD, HD), jnp.bfloat16),
            pltpu.VMEM((count, group // HD * rows), jnp.bfloat16),
            pltpu.VMEM((count, group // HD * rows), jnp.bfloat16),
            pltpu.VMEM((rows, width), jnp.float32),
            pltpu.VMEM((count, HD), jnp.float32),
            pltpu.VMEM((count, HD), jnp.float32),
        ],
        compiler_params=pltpu.CompilerParams(vmem_limit_bytes=back_limit),
        cost_estimate=pl.CostEstimate(
            flops=80 * rows * width * count, bytes_accessed=20 * rows * width, transcendentals=0
        ),
        name="backward",
    )(table, length, x, gain, cotangent, *held)


def shards(
    arriving,
    saved_input,
    returning,
    prompt_cache,
    fresh_cache,
    back_cache,
    query_gain,
    block_tables,
    fresh_lengths,
    back_lengths,
):
    cotangent = shifted_2(returning, "section", -1)
    table = block_tables[0]
    pool = collect(prompt_cache[0])
    held = chances_call(table, back_lengths, saved_input[0, 0], query_gain, pool, back_cache[0, 0])
    arriving, cotangent, inverses = lax.optimization_barrier((arriving, cotangent, held[2]))
    held = held[:2] + (inverses,) + held[3:]
    incoming = shifted_2(arriving, "section", 1)
    input_grad, pool_grad, own_grad, gain_part = backward(
        table, back_lengths, saved_input[0, 0], query_gain, pool, back_cache[0, 0], cotangent[0, 0], held
    )
    prompt_grad, gain_grad = share(pool_grad, gain_part)
    section_output = forward(
        table, fresh_lengths, incoming[0, 0], query_gain, pool, fresh_cache[0, 0]
    )
    return (
        section_output[None, None],
        input_grad[None, None],
        prompt_grad[None],
        own_grad[None, None],
        gain_grad,
    )


def solution(mesh):
    return jax.shard_map(
        shards,
        mesh=mesh,
        in_specs=(
            P("section", "fork", None, None),
            P("section", "fork", None, None),
            P("section", "fork", None, None),
            P("section", None, "fork", None),
            P("section", "fork", None, None, None),
            P("section", "fork", None, None, None),
            P("section", None),
            P("fork", None),
            P("fork"),
            P("fork"),
        ),
        out_specs=(
            P("section", "fork", None, None),
            P("section", "fork", None, None),
            P("section", None, "fork", None),
            P("section", "fork", None, None, None),
            P("section", None),
        ),
        check_vma=False,
    )
```
